32 devices in a mesh: outer: 8 (over z, x), dp: 2 (over y), mp: 2 (over core).
Axes of the slice: x: 2, y: 2, z: 4, core: 2. Of those that a mesh axis runs over, the one named last changes fastest.
Arguments:
- step_index: int32 [], replicated, may hold values from 0 to 4095
- token_ids: int32 [8, 1024], P('outer', 'dp'), may hold values from 0 to 128255, as said below
- features: bfloat16 [8, 1024, 4096], P('outer', 'dp'), may hold values from -6 to 6
- cotangent: bfloat16 [8, 1024, 2048], P('outer', 'dp', 'mp'), may hold values from -6 to 6
- weight: float32 [8, 4096, 2048], P('outer', 'dp', 'mp'), may hold values from -0.09375 to 0.09375
- momentum: float32 [8, 4096, 2048], P('outer', 'dp', 'mp'), may hold values from -0.3 to 0.3
Outputs:
- input_grad: bfloat16 [8, 1024, 4096], P('outer', 'dp')
- new_weight: float32 [8, 4096, 2048], P('outer', 'dp', 'mp')
- new_momentum: float32 [8, 4096, 2048], P('outer', 'dp', 'mp')
The draws below stay inside these ranges and needn't reach their ends.
Inputs may be any that keep to these rules, and one draw needn't show every extreme that they name: `token_ids`: the id 128004 marks padding at the end of some blocks of 512 tokens; a quarter of the tokens or so are padding.
All inputs are finite; a program needn't handle non-finite values.
Results may differ from the reference program's by a relative error of at most 0.0049.
Values may be sent and summed in bfloat16 or wider, within the bound.
No kernel may reach another device: no remote copies, remote signals or barrier semaphores. Data moves between devices by JAX's collectives and lax.ppermute only.
A program may use at most 128 MiB of HBM per device.

```python
import jax
import jax.numpy as jnp
from jax import lax

D = 4096
VOCAB = 128256
TOK_DEV = 512
KVW = 2048
POD_TOKENS = 1024
N_OUTER = 8


def draw_token_ids(key, part):
    key_ids, key_tail = jax.random.split(key)
    blocks = POD_TOKENS // TOK_DEV
    token_vals = jax.random.randint(key_ids, (N_OUTER, blocks, TOK_DEV), 0, VOCAB, dtype=jnp.int32)
    pad_len = jax.random.randint(key_tail, (N_OUTER, blocks, 1), 0, TOK_DEV // 2 + 1, dtype=jnp.int32)
    offset = jnp.arange(TOK_DEV, dtype=jnp.int32)[None, None, :]
    padded = offset >= TOK_DEV - pad_len
    token_vals = jnp.where(padded, jnp.int32(128004), token_vals)
    return token_vals.reshape(N_OUTER, POD_TOKENS)


def steps_of(key, dims, cuts, smallest, largest):
    factor_of, own = 1.0, jax.random.fold_in(key, 6)
    for dim, shards_of in cuts:
        steps = jnp.exp(jax.random.uniform(jax.random.fold_in(own, dim), (shards_of,), jnp.float32, smallest / len(cuts), largest / len(cuts)))
        factor_of = factor_of * jnp.repeat(steps, dims[dim] // shards_of).reshape([-1 if axis == dim else 1 for axis in range(len(dims))])
    return factor_of


def normal_values(key, extent, width, bound, cuts=(), kind=jnp.bfloat16):
    entries = width * jax.random.normal(key, extent, jnp.float32)
    if cuts:
        entries = entries * steps_of(key, extent, cuts, -0.22, 0.18)
    return jnp.clip(entries, -bound, bound).astype(kind)


def setup_inputs(seed: int = 0) -> dict:
    arg_keys = jax.random.split(jax.random.key(seed), 7)
    return {
        "step_index": jax.random.randint(arg_keys[0], (), 0, 4096).astype(jnp.int32),
        "token_ids": draw_token_ids(jax.random.fold_in(arg_keys[6], 71), 0),
        "features": normal_values(arg_keys[2], (N_OUTER, POD_TOKENS, D), 1.0, 6.0, ((0, 8), (1, 2))),
        "cotangent": normal_values(arg_keys[3], (N_OUTER, POD_TOKENS, KVW), 1.0, 6.0, ((0, 8), (1, 2), (2, 2))),
        "weight": normal_values(arg_keys[4], (N_OUTER, D, KVW), D ** -0.5, 0.09375, ((0, 8), (1, 2), (2, 2)), jnp.float32),
        "momentum": normal_values(arg_keys[5], (N_OUTER, D, KVW), 0.05, 0.3, ((0, 8), (1, 2), (2, 2)), jnp.float32),
    }


pad_token = 128004
peak_rate = 0.1
warm_steps = 4096.0
momentum_keep = 0.9


def reference(step_index, token_ids, features, cotangent, weight, momentum):
    keep_mask = (token_ids != pad_token)[..., None]
    masked = jnp.where(keep_mask, cotangent, jnp.zeros_like(cotangent))
    weight_half = weight.astype(jnp.bfloat16)

    def one_pod(pod_args):
        pod_x, pod_cot, pod_w = pod_args
        gradient = jnp.dot(pod_x.T, pod_cot, preferred_element_type=jnp.float32)
        input_grad = jnp.dot(pod_cot, pod_w.T, preferred_element_type=jnp.float32).astype(jnp.bfloat16)
        return gradient, input_grad

    gradients, input_grads = lax.map(one_pod, (features, masked, weight_half))
    gradients = gradients / POD_TOKENS
    rate = peak_rate * (step_index + 1).astype(jnp.float32) / warm_steps
    velocity = momentum_keep * momentum + gradients
    stepped = weight - rate * velocity
    bit_count = N_OUTER.bit_length() - 1
    shift_by = (step_index % bit_count).astype(jnp.int32)
    partner = jnp.bitwise_xor(jnp.arange(N_OUTER, dtype=jnp.int32), jnp.left_shift(jnp.ones((), jnp.int32), shift_by))
    new_weight = 0.5 * (stepped + stepped[partner])
    new_momentum = 0.5 * (velocity + velocity[partner])
    return input_grads, new_weight, new_momentum
```

```python
import functools

import jax
import jax.numpy as jnp
from jax import lax
from jax.experimental import pallas as pl
from jax.experimental.pallas import tpu as pltpu
from jax.sharding import PartitionSpec as P

pad_token = 128004
peak_rate = 0.1
warm_steps = 4096.0
momentum_keep = 0.9

weight_parts = (2, 14)
velocity_parts = (8, 4, 2, 1, 1)
params = pltpu.CompilerParams(vmem_limit_bytes=40 * 1024 * 1024)


def shifted(value, axis, by):
    n = lax.axis_size(axis)
    return lax.ppermute(value, axis, [(s, (s + by) % n) for s in range(n)])


def from_partner(value, bit):
    n = lax.axis_size("outer")
    return lax.ppermute(value, "outer", [(s, s ^ (1 << bit)) for s in range(n)])


def starts_of(parts, rows):
    out, at, upto = [], 0, 0
    for part in parts:
        upto += part
        end = -(-rows * upto // (16 * 128)) * 128
        if end > at:
            out.append((at, end - at))
        at = end
    return out


def fitting(largest, *sizes):
    block = largest
    while any(size % block for size in sizes):
        block //= 2
    return block


def cost(flops, nbytes):
    return pl.CostEstimate(flops=int(flops), bytes_accessed=int(nbytes), transcendentals=0)


def velocity_kernel(n, scale, where_ref, *refs):
    xs, ms, old_ref, v_ref, short_ref = refs[:n], refs[n : 2 * n], refs[2 * n], refs[2 * n + 1], refs[2 * n + 2]
    total = None
    for x_ref, m_ref in zip(xs, ms):
        term = lax.dot_general(
            x_ref[...], m_ref[...], (((0,), (0,)), ((), ())), preferred_element_type=jnp.float32
        )
        total = term if total is None else total + term
    v = momentum_keep * old_ref[...] + total * scale
    v_ref[...] = v
    short_ref[...] = v.astype(jnp.bfloat16)


def velocity_rows(dp_at, activation, others, masks, momentum, first, size, tokens):
    rows, cols = momentum.shape
    toks = activation.shape[0]
    n = len(masks)
    block = fitting(256, first, size)
    per_dev, skip = rows // block, first // block
    return pl.pallas_call(
        functools.partial(velocity_kernel, n, 1.0 / tokens),
        grid_spec=pltpu.PrefetchScalarGridSpec(
            num_scalar_prefetch=1,
            grid=(size // block,),
            in_specs=[pl.BlockSpec((toks, block), lambda r, at: (0, at[0] * per_dev + skip + r))]
            + [pl.BlockSpec((toks, block), lambda r, at: (0, skip + r))] * (n - 1)
            + [pl.BlockSpec((toks, cols), lambda r, at: (0, 0))] * n
            + [pl.BlockSpec((block, cols), lambda r, at: (skip + r, 0))],
            out_specs=[pl.BlockSpec((block, cols), lambda r, at: (r, 0))] * 2,
        ),
        out_shape=[
            jax.ShapeDtypeStruct((size, cols), jnp.float32),
            jax.ShapeDtypeStruct((size, cols), jnp.bfloat16),
        ],
        compiler_params=params,
        cost_estimate=cost(2 * n * toks * size * cols, size * cols * 10 + n * toks * (size + cols) * 2),
        name="velocity_rows",
    )(dp_at, activation, *others, *masks, momentum)


def term_kernel(where_ref, m_ref, w_ref, out_ref):
    out_ref[...] = lax.dot_general(
        m_ref[...],
        w_ref[...].astype(jnp.bfloat16),
        (((1,), (1,)), ((), ())),
        preferred_element_type=jnp.float32,
    )


def sum_kernel(where_ref, m_ref, w_ref, add_ref, out_ref):
    term = lax.dot_general(
        m_ref[...],
        w_ref[...].astype(jnp.bfloat16),
        (((1,), (1,)), ((), ())),
        preferred_element_type=jnp.float32,
    )
    out_ref[...] = (term + add_ref[...]).astype(jnp.bfloat16)


def term_rows(part, mask, weight, added=None):
    rows, cols = weight.shape
    toks = mask.shape[0]
    half = rows // 2
    block = fitting(256, half)
    steps = half // block
    kernel, kind, extra_specs, extra = term_kernel, jnp.float32, [], []
    if added is not None:
        kernel, kind, extra = sum_kernel, jnp.bfloat16, [added]
        extra_specs = [pl.BlockSpec((toks, block), lambda r, at: (0, r))]
    return pl.pallas_call(
        kernel,
        grid_spec=pltpu.PrefetchScalarGridSpec(
            num_scalar_prefetch=1,
            grid=(steps,),
            in_specs=[
                pl.BlockSpec((toks, cols), lambda r, at: (0, 0)),
                pl.BlockSpec((block, cols), lambda r, at: (at[0] * steps + r, 0)),
            ]
            + extra_specs,
            out_specs=pl.BlockSpec((toks, block), lambda r, at: (0, r)),
        ),
        out_shape=jax.ShapeDtypeStruct((toks, half), kind),
        compiler_params=params,
        cost_estimate=cost(2 * toks * half * cols, half * cols * 4 + toks * cols * 2 + toks * half * 6),
        name="term_rows",
    )(part, mask, weight, *extra)


def half_kernel(w_ref, peer_ref, *refs):
    refs[-1][...] = 0.5 * (w_ref[...] + peer_ref[...].astype(jnp.float32))


def half_rows(weight, peer, first, into):
    rows, cols = weight.shape
    size = peer.shape[0]
    block = fitting(256, first, size)
    skip = first // block
    whole_spec = pl.BlockSpec((block, cols), lambda r: (skip + r, 0))
    in_specs = [whole_spec, pl.BlockSpec((block, cols), lambda r: (r, 0))]
    extra, aliases = [], {}
    if into is not None:
        in_specs.append(pl.BlockSpec(memory_space=pl.ANY))
        extra, aliases = [into], {2: 0}
    return pl.pallas_call(
        half_kernel,
        grid=(size // block,),
        in_specs=in_specs,
        out_specs=whole_spec,
        out_shape=jax.ShapeDtypeStruct((rows, cols), jnp.float32),
        input_output_aliases=aliases,
        compiler_params=params,
        cost_estimate=cost(2 * size * cols, size * cols * 10),
        name="half_rows",
    )(weight, peer, *extra)


def final_kernel(rate_ref, v_ref, peer_ref, half_ref, *refs):
    new_weight_ref, new_momentum_ref = refs[-2], refs[-1]
    mean = 0.5 * (v_ref[...] + peer_ref[...].astype(jnp.float32))
    new_momentum_ref[...] = mean
    new_weight_ref[...] = half_ref[...] - rate_ref[0] * mean


def final_rows(rate, v, peer, half, into, first):
    rows, cols = half.shape
    size = v.shape[0]
    block = fitting(128, first, size)
    skip = first // block
    part_spec = pl.BlockSpec((block, cols), lambda r: (r, 0))
    whole_spec = pl.BlockSpec((block, cols), lambda r: (skip + r, 0))
    in_specs = [pl.BlockSpec(memory_space=pltpu.SMEM), part_spec, part_spec, whole_spec]
    extra, aliases = [], {3: 0}
    if into is not None:
        in_specs.append(pl.BlockSpec(memory_space=pl.ANY))
        extra, aliases = [into], {3: 0, 4: 1}
    return pl.pallas_call(
        final_kernel,
        grid=(size // block,),
        in_specs=in_specs,
        out_specs=[whole_spec, whole_spec],
        out_shape=[jax.ShapeDtypeStruct((rows, cols), jnp.float32)] * 2,
        input_output_aliases=aliases,
        compiler_params=params,
        cost_estimate=cost(4 * size * cols, size * cols * 18),
        name="final_rows",
    )(rate, v, peer, half, *extra)


def step_with(bit, step_index, token_ids, activation, cotangent, weight, momentum):
    rows, cols = weight.shape
    toks, width = activation.shape
    n_dp = lax.axis_size("dp")
    dp, mp = lax.axis_index("dp"), lax.axis_index("mp")
    half = rows // 2
    rate = peak_rate * (step_index + 1).astype(jnp.float32) / warm_steps

    weight_peers = []
    for first, size in starts_of(weight_parts, rows):
        short = weight[first : first + size].astype(jnp.bfloat16)
        weight_peers.append((first, from_partner(short, bit)))

    keep = (token_ids != pad_token)[:, None]
    masked = jnp.where(keep, cotangent, jnp.zeros_like(cotangent))
    masks = [masked] + [shifted(masked, "dp", k) for k in range(1, n_dp)]

    others = []
    for k in range(1, n_dp):
        to = lax.rem(dp + k, n_dp)
        sent = lax.dynamic_slice(activation, (0, to * rows + mp * half), (toks, half))
        mine = shifted(sent, "dp", k)
        other = shifted(mine, "mp", 1)
        others.append(
            jnp.where(mp == 0, jnp.concatenate([mine, other], 1), jnp.concatenate([other, mine], 1))
        )

    dp_at = dp.astype(jnp.int32)[None]
    velocities = []
    for first, size in starts_of(velocity_parts, rows):
        v, short = velocity_rows(dp_at, activation, others, masks, momentum, first, size, toks * n_dp)
        velocities.append((first, v, from_partner(short, bit)))

    keep_part = mp.astype(jnp.int32)[None]
    give_part = 1 - keep_part
    input_grad = jnp.zeros((toks, width), jnp.bfloat16)
    for k in reversed(range(n_dp)):
        given = shifted(term_rows(give_part, masks[k], weight), "mp", 1)
        done = term_rows(keep_part, masks[k], weight, given)
        if k:
            done = shifted(done, "dp", n_dp - k)
        other = shifted(done, "mp", 1)
        base = lax.rem(dp + k, n_dp) * rows
        input_grad = lax.dynamic_update_slice(input_grad, done, (0, base + mp * half))
        input_grad = lax.dynamic_update_slice(input_grad, other, (0, base + (1 - mp) * half))

    new_weight, new_momentum = None, None
    for first, peer in weight_peers:
        new_weight = half_rows(weight, peer, first, new_weight)
    for first, v, peer in velocities:
        new_weight, new_momentum = final_rows(rate[None], v, peer, new_weight, new_momentum, first)
    return input_grad, new_weight, new_momentum


def on_device(step_index, token_ids, features, cotangent, weight, momentum):
    bit_count = lax.axis_size("outer").bit_length() - 1
    outs = lax.switch(
        step_index % bit_count,
        [functools.partial(step_with, bit) for bit in range(bit_count)],
        step_index,
        token_ids[0],
        features[0],
        cotangent[0],
        weight[0],
        momentum[0],
    )
    return tuple(out[None] for out in outs)


def solution(mesh):
    placed = (
        P(),
        P("outer", "dp"),
        P("outer", "dp", None),
        P("outer", "dp", "mp"),
        P("outer", "dp", "mp"),
        P("outer", "dp", "mp"),
    )
    return jax.shard_map(
        on_device,
        mesh=mesh,
        in_specs=placed,
        out_specs=(P("outer", "dp", None), P("outer", "dp", "mp"), P("outer", "dp", "mp")),
        check_vma=False,
    )
```

```python
import functools

import jax
import jax.numpy as jnp
from jax import lax
from jax.experimental import pallas as pl
from jax.experimental.pallas import tpu as pltpu
from jax.sharding import PartitionSpec as P

pad_token = 128004
peak_rate = 0.1
warm_steps = 4096.0
momentum_keep = 0.9

velocity_parts = (10, 4, 1, 1)

any_spec = pl.BlockSpec(memory_space=pl.ANY)


def shifted(value, axis, by):
    n = lax.axis_size(axis)
    return lax.ppermute(value, axis, [(s, (s + by) % n) for s in range(n)])


def from_partner(value, bit):
    n = lax.axis_size("outer")
    return lax.ppermute(value, "outer", [(s, s ^ (1 << bit)) for s in range(n)])


def starts_of(parts, rows):
    out, at, upto = [], 0, 0
    for part in parts:
        upto += part
        end = -(-rows * upto // (16 * 128)) * 128
        if end > at:
            out.append((at, end - at))
        at = end
    return out


def fitting(largest, *sizes):
    block = largest
    while any(size % block for size in sizes):
        block //= 2
    return block


class Chain:
    def __init__(self):
        self.token = None

    def call(self, kernel, name, grid, places, ins, outs, aliases=()):
        ins = list(ins)
        n_out = len(outs)
        if self.token is not None:
            ins.append((self.token, any_spec))
        n_in = len(ins)

        def body(place_ref, *refs):
            kernel(place_ref, refs[:n_in], refs[n_in : n_in + n_out])

        got = pl.pallas_call(
            body,
            grid_spec=pltpu.PrefetchScalarGridSpec(
                num_scalar_prefetch=1,
                grid=grid,
                in_specs=[spec for _, spec in ins],
                out_specs=[spec for _, _, spec in outs] + [any_spec],
            ),
            out_shape=[jax.ShapeDtypeStruct(shape, kind) for shape, kind, _ in outs]
            + [jax.ShapeDtypeStruct((8, 128), jnp.float32)],
            input_output_aliases={i + 1: o for i, o in aliases},
            compiler_params=pltpu.CompilerParams(vmem_limit_bytes=63 * 1024 * 1024),
            cost_estimate=pl.CostEstimate(flops=0, bytes_accessed=0, transcendentals=0),
            name=name,
        )(places, *[array for array, _ in ins])
        self.token = got[-1]
        return got[:-1]


def cast_kernel(places, ins, outs):
    outs[0][...] = ins[0][...].astype(outs[0].dtype)


def cast_rows(chain, places, weight):
    rows, cols = weight.shape
    block = fitting(256, rows)
    spec = pl.BlockSpec((block, cols), lambda r, at: (r, 0))
    return chain.call(
        cast_kernel,
        "cast_rows",
        (rows // block,),
        places,
        [(weight, spec)],
        [((rows, cols), jnp.bfloat16, spec)],
    )[0]


def mask_kernel(places, ins, outs):
    ids, cot = ins[0], ins[1]
    rows, cols = cot.shape
    turned = jnp.broadcast_to(ids[...], (128, rows)).T
    keep = turned != pad_token
    for at in range(0, cols, 128):
        value = cot[:, at : at + 128]
        outs[0][:, at : at + 128] = jnp.where(keep, value, jnp.zeros_like(value))


def mask_rows(chain, places, ids, cot):
    rows, cols = cot.shape
    block = fitting(256, rows)
    return chain.call(
        mask_kernel,
        "mask_rows",
        (rows // block,),
        places,
        [
            (ids, pl.BlockSpec((1, block), lambda r, at: (0, r))),
            (cot, pl.BlockSpec((block, cols), lambda r, at: (r, 0))),
        ],
        [((rows, cols), cot.dtype, pl.BlockSpec((block, cols), lambda r, at: (r, 0)))],
    )[0]


def take_columns(chain, places, features, by, n, half):
    toks = features.shape[0]
    block = fitting(256, toks)
    return chain.call(
        cast_kernel,
        "take_columns",
        (toks // block,),
        places,
        [
            (
                features,
                pl.BlockSpec((block, half), lambda r, at: (r, 2 * lax.rem(at[0] + by, n) + at[1])),
            )
        ],
        [((toks, half), features.dtype, pl.BlockSpec((block, half), lambda r, at: (r, 0)))],
    )[0]


def take_rows(chain, places, short):
    half, cols = short.shape[0] // 2, short.shape[1]
    block = fitting(512, half)
    steps = half // block
    return chain.call(
        cast_kernel,
        "take_rows",
        (steps,),
        places,
        [(short, pl.BlockSpec((block, cols), lambda r, at: ((1 - at[1]) * steps + r, 0)))],
        [((half, cols), short.dtype, pl.BlockSpec((block, cols), lambda r, at: (r, 0)))],
    )[0]


def velocity_kernel(n, scale, places, ins, outs):
    total = None
    for x_ref, m_ref in zip(ins[:n], ins[n : 2 * n]):
        term = lax.dot_general(
            x_ref[...], m_ref[...], (((0,), (0,)), ((), ())), preferred_element_type=jnp.float32
        )
        total = term if total is None else total + term
    v = momentum_keep * ins[2 * n][...] + total * scale
    outs[0][...] = v
    outs[1][...] = v.astype(jnp.bfloat16)


def velocity_rows(chain, places, activation, others, masks, momentum, first, size):
    rows, cols = momentum.shape
    toks = activation.shape[0]
    n = len(masks)
    block = fitting(256, first, size)
    per_dev, skip = rows // block, first // block
    row_spec = pl.BlockSpec((block, cols), lambda r, at: (r, 0))
    return chain.call(
        functools.partial(velocity_kernel, n, 1.0 / (toks * n)),
        "velocity_rows",
        (size // block,),
        places,
        [(activation, pl.BlockSpec((toks, block), lambda r, at: (0, at[0] * per_dev + skip + r)))]
        + [(x, pl.BlockSpec((toks, block), lambda r, at: (0, skip + r))) for x in others]
        + [(m, pl.BlockSpec((toks, cols), lambda r, at: (0, 0))) for m in masks]
        + [(momentum, pl.BlockSpec((block, cols), lambda r, at: (skip + r, 0)))],
        [((size, cols), jnp.float32, row_spec), ((size, cols), jnp.bfloat16, row_spec)],
    )


def input_kernel(places, ins, outs):
    own, other = (
        lax.dot_general(
            ins[at][...], ins[at + 1][...], (((1,), (1,)), ((), ())), preferred_element_type=jnp.float32
        )
        for at in (0, 2)
    )
    outs[0][...] = (own + other).astype(outs[0].dtype)


def input_columns(chain, places, mask, short, mask_other, short_other):
    half, cols = short_other.shape
    toks = mask.shape[0]
    block = fitting(256, half)
    steps = half // block
    mask_spec = pl.BlockSpec((toks, cols), lambda r, at: (0, 0))
    return chain.call(
        input_kernel,
        "input_columns",
        (steps,),
        places,
        [
            (mask, mask_spec),
            (short, pl.BlockSpec((block, cols), lambda r, at: (at[1] * steps + r, 0))),
            (mask_other, mask_spec),
            (short_other, pl.BlockSpec((block, cols), lambda r, at: (r, 0))),
        ],
        [((toks, half), jnp.bfloat16, pl.BlockSpec((toks, block), lambda r, at: (0, r)))],
    )[0]


def join_kernel(n, places, ins, outs):
    column = pl.program_id(0)
    by = lax.rem(column // 2 - places[0] + n, n)
    piece = 2 * by + jnp.where(lax.rem(column, 2) == places[1], 0, 1)
    for at in range(2 * n):

        @pl.when(piece == at)
        def _():
            outs[0][...] = ins[at][...]


def join_columns(chain, places, pieces):
    toks, width = pieces[0].shape
    return chain.call(
        functools.partial(join_kernel, len(pieces) // 2),
        "join_columns",
        (len(pieces),),
        places,
        [(piece, pl.BlockSpec((toks, width), lambda c, at: (0, 0))) for piece in pieces],
        [
            (
                (toks, width * len(pieces)),
                pieces[0].dtype,
                pl.BlockSpec((toks, width), lambda c, at: (0, c)),
            )
        ],
    )[0]


def half_kernel(places, ins, outs):
    outs[0][...] = 0.5 * (ins[0][...] + ins[1][...].astype(jnp.float32))


def half_rows(chain, places, weight, peer):
    rows, cols = weight.shape
    block = fitting(256, rows)
    spec = pl.BlockSpec((block, cols), lambda r, at: (r, 0))
    return chain.call(
        half_kernel,
        "half_rows",
        (rows // block,),
        places,
        [(weight, spec), (peer, spec)],
        [((rows, cols), jnp.float32, spec)],
    )[0]


def final_kernel(places, ins, outs):
    mean = 0.5 * (ins[0][...] + ins[1][...].astype(jnp.float32))
    outs[1][...] = mean
    outs[0][...] = ins[2][...] - ins[3][0] * mean


def final_rows(chain, places, rate, v, peer, half, into, first):
    rows, cols = half.shape
    size = v.shape[0]
    block = fitting(256, first, size)
    skip = first // block
    part_spec = pl.BlockSpec((block, cols), lambda r, at: (r, 0))
    whole_spec = pl.BlockSpec((block, cols), lambda r, at: (skip + r, 0))
    ins = [
        (v, part_spec),
        (peer, part_spec),
        (half, whole_spec),
        (rate, pl.BlockSpec(memory_space=pltpu.SMEM)),
    ]
    aliases = [(2, 0)]
    if into is not None:
        aliases.append((len(ins), 1))
        ins.append((into, any_spec))
    return chain.call(
        final_kernel,
        "final_rows",
        (size // block,),
        places,
        ins,
        [((rows, cols), jnp.float32, whole_spec)] * 2,
        aliases,
    )


def step_with(bit, places, rate, ids, activation, cotangent, weight, momentum):
    rows = weight.shape[0]
    n_dp = lax.axis_size("dp")
    mp = places[1]
    half = rows // 2
    chain = Chain()

    short = cast_rows(chain, places, weight)
    weight_peer = from_partner(short, bit)

    masked = mask_rows(chain, places, ids, cotangent)
    masks = [masked] + [shifted(masked, "dp", k) for k in range(1, n_dp)]

    others = []
    for k in range(1, n_dp):
        mine = shifted(take_columns(chain, places, activation, k, n_dp, half), "dp", k)
        other = shifted(mine, "mp", 1)
        others.append(
            jnp.where(mp == 0, jnp.concatenate([mine, other], 1), jnp.concatenate([other, mine], 1))
        )

    short_other = shifted(take_rows(chain, places, short), "mp", 1)

    velocities = []
    for first, size in starts_of(velocity_parts, rows):
        v, v_short = velocity_rows(chain, places, activation, others, masks, momentum, first, size)
        velocities.append((first, v, from_partner(v_short, bit)))

    new_weight = half_rows(chain, places, weight, weight_peer)

    done = {}
    for k in reversed(range(n_dp)):
        done[k] = input_columns(
            chain, places, masks[k], short, shifted(masks[k], "mp", 1), short_other
        )
        if k:
            done[k] = shifted(done[k], "dp", n_dp - k)

    pieces = []
    for k in range(n_dp):
        pieces += [done[k], shifted(done[k], "mp", 1)]
    input_grad = join_columns(chain, places, pieces)

    new_momentum = None
    for first, v, peer in velocities:
        new_weight, new_momentum = final_rows(
            chain, places, rate, v, peer, new_weight, new_momentum, first
        )
    return input_grad, new_weight, new_momentum


def on_device(step_index, token_ids, features, cotangent, weight, momentum):
    bit_count = lax.axis_size("outer").bit_length() - 1
    places = jnp.stack([lax.axis_index("dp"), lax.axis_index("mp")]).astype(jnp.int32)
    rate = (peak_rate * (step_index + 1).astype(jnp.float32) / warm_steps)[None]
    outs = lax.switch(
        step_index % bit_count,
        [functools.partial(step_with, bit) for bit in range(bit_count)],
        places,
        rate,
        token_ids,
        features[0],
        cotangent[0],
        weight[0],
        momentum[0],
    )
    return tuple(out[None] for out in outs)


def solution(mesh):
    placed = (
        P(),
        P("outer", "dp"),
        P("outer", "dp", None),
        P("outer", "dp", "mp"),
        P("outer", "dp", "mp"),
        P("outer", "dp", "mp"),
    )
    return jax.shard_map(
        on_device,
        mesh=mesh,
        in_specs=placed,
        out_specs=(P("outer", "dp", None), P("outer", "dp", "mp"), P("outer", "dp", "mp")),
        check_vma=False,
    )
```

```python
import functools

import jax
import jax.numpy as jnp
from jax import lax
from jax.experimental import pallas as pl
from jax.experimental.pallas import tpu as pltpu
from jax.sharding import PartitionSpec as P

pad_token = 128004
peak_rate = 0.1
warm_steps = 4096.0
momentum_keep = 0.9

velocity_parts = (9, 5, 1, 1)
weight_parts = (6, 10)

any_spec = pl.BlockSpec(memory_space=pl.ANY)


def shifted(value, axis, by):
    n = lax.axis_size(axis)
    return lax.ppermute(value, axis, [(s, (s + by) % n) for s in range(n)])


def from_partner(value, bit):
    n = lax.axis_size("outer")
    return lax.ppermute(value, "outer", [(s, s ^ (1 << bit)) for s in range(n)])


def starts_of(parts, rows):
    out, at, upto = [], 0, 0
    for part in parts:
        upto += part
        end = -(-rows * upto // (16 * 128)) * 128
        if end > at:
            out.append((at, end - at))
        at = end
    return out


def fitting(largest, *sizes):
    block = largest
    while any(size % block for size in sizes):
        block //= 2
    return block


class Chain:
    def __init__(self, token=None):
        self.token = token

    def call(self, kernel, name, grid, places, ins, outs, aliases=()):
        ins = list(ins)
        n_out = len(outs)
        if self.token is not None:
            ins.append((self.token, any_spec))
        n_in = len(ins)

        def body(place_ref, *refs):
            kernel(place_ref, refs[:n_in], refs[n_in : n_in + n_out])

        got = pl.pallas_call(
            body,
            grid_spec=pltpu.PrefetchScalarGridSpec(
                num_scalar_prefetch=1,
                grid=grid,
                in_specs=[spec for _, spec in ins],
                out_specs=[spec for _, _, spec in outs] + [any_spec],
            ),
            out_shape=[jax.ShapeDtypeStruct(shape, kind) for shape, kind, _ in outs]
            + [jax.ShapeDtypeStruct((8, 128), jnp.float32)],
            input_output_aliases={i + 1: o for i, o in aliases},
            compiler_params=pltpu.CompilerParams(vmem_limit_bytes=64 * 1024 * 1024 - 128 * 1024),
            cost_estimate=pl.CostEstimate(flops=0, bytes_accessed=0, transcendentals=0),
            name=name,
        )(places, *[array for array, _ in ins])
        self.token = got[-1]
        return got[:-1]


def cast_kernel(places, ins, outs):
    outs[0][...] = ins[0][...].astype(outs[0].dtype)


def cast_rows(chain, places, weight, first, size):
    cols = weight.shape[1]
    block = fitting(512, first, size) if first else fitting(size, size)
    if block > 512:
        block = fitting(block // 2, size)
    skip = first // block
    return chain.call(
        cast_kernel,
        "cast_rows",
        (size // block,),
        places,
        [(weight, pl.BlockSpec((block, cols), lambda r, at: (skip + r, 0)))],
        [((size, cols), jnp.bfloat16, pl.BlockSpec((block, cols), lambda r, at: (r, 0)))],
    )[0]


def mask_kernel(places, ins, outs):
    ids, cot = ins[0], ins[1]
    rows, cols = cot.shape
    turned = jnp.broadcast_to(ids[...], (128, rows)).T
    keep = turned != pad_token
    for at in range(0, cols, 128):
        value = cot[:, at : at + 128]
        outs[0][:, at : at + 128] = jnp.where(keep, value, jnp.zeros_like(value))


def mask_rows(chain, places, ids, cot):
    rows, cols = cot.shape
    block = fitting(256, rows)
    return chain.call(
        mask_kernel,
        "mask_rows",
        (rows // block,),
        places,
        [
            (ids, pl.BlockSpec((1, block), lambda r, at: (0, r))),
            (cot, pl.BlockSpec((block, cols), lambda r, at: (r, 0))),
        ],
        [((rows, cols), cot.dtype, pl.BlockSpec((block, cols), lambda r, at: (r, 0)))],
    )[0]


def take_columns(chain, places, features, by, n, half):
    toks = features.shape[0]
    block = fitting(256, toks)
    return chain.call(
        cast_kernel,
        "take_columns",
        (toks // block,),
        places,
        [
            (
                features,
                pl.BlockSpec((block, half), lambda r, at: (r, 2 * lax.rem(at[0] + by, n) + at[1])),
            )
        ],
        [((toks, half), features.dtype, pl.BlockSpec((block, half), lambda r, at: (r, 0)))],
    )[0]


def take_rows(chain, places, weight):
    half, cols = weight.shape[0] // 2, weight.shape[1]
    block = fitting(512, half)
    steps = half // block
    return chain.call(
        cast_kernel,
        "take_rows",
        (steps,),
        places,
        [(weight, pl.BlockSpec((block, cols), lambda r, at: ((1 - at[1]) * steps + r, 0)))],
        [((half, cols), jnp.bfloat16, pl.BlockSpec((block, cols), lambda r, at: (r, 0)))],
    )[0]


def velocity_kernel(n, scale, places, ins, outs):
    total = None
    for x_ref, m_ref in zip(ins[:n], ins[n : 2 * n]):
        term = lax.dot_general(
            x_ref[...], m_ref[...], (((0,), (0,)), ((), ())), preferred_element_type=jnp.float32
        )
        total = term if total is None else total + term
    v = momentum_keep * ins[2 * n][...] + total * scale
    outs[0][...] = v
    outs[1][...] = v.astype(jnp.bfloat16)


def velocity_rows(chain, places, activation, others, masks, momentum, first, size):
    rows, cols = momentum.shape
    toks = activation.shape[0]
    n = len(masks)
    block = fitting(256, first, size)
    per_dev, skip = rows // block, first // block
    row_spec = pl.BlockSpec((block, cols), lambda r, at: (r, 0))
    return chain.call(
        functools.partial(velocity_kernel, n, 1.0 / (toks * n)),
        "velocity_rows",
        (size // block,),
        places,
        [(activation, pl.BlockSpec((toks, block), lambda r, at: (0, at[0] * per_dev + skip + r)))]
        + [(x, pl.BlockSpec((toks, block), lambda r, at: (0, skip + r))) for x in others]
        + [(m, pl.BlockSpec((toks, cols), lambda r, at: (0, 0))) for m in masks]
        + [(momentum, pl.BlockSpec((block, cols), lambda r, at: (skip + r, 0)))],
        [((size, cols), jnp.float32, row_spec), ((size, cols), jnp.bfloat16, row_spec)],
    )


def input_kernel(places, ins, outs):
    own, other = (
        lax.dot_general(
            ins[at][...],
            ins[at + 1][...].astype(jnp.bfloat16),
            (((1,), (1,)), ((), ())),
            preferred_element_type=jnp.float32,
        )
        for at in (0, 2)
    )
    outs[0][...] = (own + other).astype(outs[0].dtype)


def input_columns(chain, places, mask, weight, mask_other, short_other):
    half, cols = short_other.shape
    toks = mask.shape[0]
    block = fitting(256, half)
    steps = half // block
    mask_spec = pl.BlockSpec((toks, cols), lambda r, at: (0, 0))
    return chain.call(
        input_kernel,
        "input_columns",
        (steps,),
        places,
        [
            (mask, mask_spec),
            (weight, pl.BlockSpec((block, cols), lambda r, at: (at[1] * steps + r, 0))),
            (mask_other, mask_spec),
            (short_other, pl.BlockSpec((block, cols), lambda r, at: (r, 0))),
        ],
        [((toks, half), jnp.bfloat16, pl.BlockSpec((toks, block), lambda r, at: (0, r)))],
    )[0]


def join_kernel(n, places, ins, outs):
    column = pl.program_id(0)
    by = lax.rem(column // 2 - places[0] + n, n)
    piece = 2 * by + jnp.where(lax.rem(column, 2) == places[1], 0, 1)
    for at in range(2 * n):

        @pl.when(piece == at)
        def _():
            outs[0][...] = ins[at][...]


def join_columns(chain, places, pieces):
    toks, width = pieces[0].shape
    return chain.call(
        functools.partial(join_kernel, len(pieces) // 2),
        "join_columns",
        (len(pieces),),
        places,
        [(piece, pl.BlockSpec((toks, width), lambda c, at: (0, 0))) for piece in pieces],
        [
            (
                (toks, width * len(pieces)),
                pieces[0].dtype,
                pl.BlockSpec((toks, width), lambda c, at: (0, c)),
            )
        ],
    )[0]


def half_kernel(places, ins, outs):
    outs[0][...] = 0.5 * (ins[0][...] + ins[1][...].astype(jnp.float32))


def half_rows(chain, places, weight, peer, first, into):
    rows, cols = weight.shape
    size = peer.shape[0]
    block = fitting(512, first, size)
    skip = first // block
    whole_spec = pl.BlockSpec((block, cols), lambda r, at: (skip + r, 0))
    ins = [(weight, whole_spec), (peer, pl.BlockSpec((block, cols), lambda r, at: (r, 0)))]
    aliases = []
    if into is not None:
        aliases = [(len(ins), 0)]
        ins.append((into, any_spec))
    return chain.call(
        half_kernel,
        "half_rows",
        (size // block,),
        places,
        ins,
        [((rows, cols), jnp.float32, whole_spec)],
        aliases,
    )[0]


def final_kernel(places, ins, outs):
    mean = 0.5 * (ins[0][...] + ins[1][...].astype(jnp.float32))
    outs[1][...] = mean
    outs[0][...] = ins[2][...] - ins[3][0] * mean


def final_rows(chain, places, rate, v, peer, half, into, first):
    rows, cols = half.shape
    size = v.shape[0]
    block = fitting(256, first, size)
    skip = first // block
    part_spec = pl.BlockSpec((block, cols), lambda r, at: (r, 0))
    whole_spec = pl.BlockSpec((block, cols), lambda r, at: (skip + r, 0))
    ins = [
        (v, part_spec),
        (peer, part_spec),
        (half, whole_spec),
        (rate, pl.BlockSpec(memory_space=pltpu.SMEM)),
    ]
    aliases = [(2, 0)]
    if into is not None:
        aliases.append((len(ins), 1))
        ins.append((into, any_spec))
    return chain.call(
        final_kernel,
        "final_rows",
        (size // block,),
        places,
        ins,
        [((rows, cols), jnp.float32, whole_spec)] * 2,
        aliases,
    )


def step_with(bit, token, first_short, places, rate, ids, activation, cotangent, weight, momentum):
    rows = weight.shape[0]
    n_dp = lax.axis_size("dp")
    mp = places[1]
    half = rows // 2
    chain = Chain(token)

    weight_pieces = starts_of(weight_parts, rows)
    weight_peers = [from_partner(first_short, bit)]
    for first, size in weight_pieces[1:]:
        weight_peers.append(from_partner(cast_rows(chain, places, weight, first, size), bit))

    masked = mask_rows(chain, places, ids, cotangent)
    masks = [masked] + [shifted(masked, "dp", k) for k in range(1, n_dp)]

    others = []
    for k in range(1, n_dp):
        mine = shifted(take_columns(chain, places, activation, k, n_dp, half), "dp", k)
        other = shifted(mine, "mp", 1)
        others.append(
            jnp.where(mp == 0, jnp.concatenate([mine, other], 1), jnp.concatenate([other, mine], 1))
        )

    new_weight = half_rows(chain, places, weight, weight_peers[0], 0, None)
    short_other = shifted(take_rows(chain, places, weight), "mp", 1)

    velocities = []
    for first, size in starts_of(velocity_parts, rows):
        v, v_short = velocity_rows(chain, places, activation, others, masks, momentum, first, size)
        velocities.append((first, v, from_partner(v_short, bit)))

    for (first, _), peer in zip(weight_pieces[1:], weight_peers[1:]):
        new_weight = half_rows(chain, places, weight, peer, first, new_weight)

    done = {}
    for k in reversed(range(n_dp)):
        done[k] = input_columns(
            chain, places, masks[k], weight, shifted(masks[k], "mp", 1), short_other
        )
        if k:
            done[k] = shifted(done[k], "dp", n_dp - k)

    pieces = []
    for k in range(n_dp):
        pieces += [done[k], shifted(done[k], "mp", 1)]
    input_grad = join_columns(chain, places, pieces)

    new_momentum = None
    for first, v, peer in velocities:
        new_weight, new_momentum = final_rows(
            chain, places, rate, v, peer, new_weight, new_momentum, first
        )
    return input_grad, new_weight, new_momentum


def on_device(step_index, token_ids, features, cotangent, weight, momentum):
    bit_count = lax.axis_size("outer").bit_length() - 1
    places = jnp.stack([lax.axis_index("dp"), lax.axis_index("mp")]).astype(jnp.int32)
    rate = (peak_rate * (step_index + 1).astype(jnp.float32) / warm_steps)[None]
    chain = Chain()
    first, size = starts_of(weight_parts, weight.shape[1])[0]
    first_short = cast_rows(chain, places, weight[0], first, size)
    outs = lax.switch(
        step_index % bit_count,
        [functools.partial(step_with, bit) for bit in range(bit_count)],
        chain.token,
        first_short,
        places,
        rate,
        token_ids,
        features[0],
        cotangent[0],
        weight[0],
        momentum[0],
    )
    return tuple(out[None] for out in outs)


def solution(mesh):
    placed = (
        P(),
        P("outer", "dp"),
        P("outer", "dp", None),
        P("outer", "dp", "mp"),
        P("outer", "dp", "mp"),
        P("outer", "dp", "mp"),
    )
    return jax.shard_map(
        on_device,
        mesh=mesh,
        in_specs=placed,
        out_specs=(P("outer", "dp", None), P("outer", "dp", "mp"), P("outer", "dp", "mp")),
        check_vma=False,
    )
```

```python
import functools

import jax
import jax.numpy as jnp
from jax import lax
from jax.experimental import pallas as pl
from jax.experimental.pallas import tpu as pltpu
from jax.sharding import PartitionSpec as P

pad_token = 128004
peak_rate = 0.1
warm_steps = 4096.0
momentum_keep = 0.9

velocity_parts = (9, 5, 1, 1)
weight_parts = (6, 10)

any_spec = pl.BlockSpec(memory_space=pl.ANY)


def shifted(value, axis, by):
    n = lax.axis_size(axis)
    return lax.ppermute(value, axis, [(s, (s + by) % n) for s in range(n)])


def from_partner(value, bit):
    n = lax.axis_size("outer")
    return lax.ppermute(value, "outer", [(s, s ^ (1 << bit)) for s in range(n)])


def starts_of(parts, rows):
    out, at, upto = [], 0, 0
    for part in parts:
        upto += part
        end = -(-rows * upto // (16 * 128)) * 128
        if end > at:
            out.append((at, end - at))
        at = end
    return out


def fitting(largest, *sizes):
    block = largest
    while any(size % block for size in sizes):
        block //= 2
    return block


def by_slabs(ref, body):
    rows = ref.shape[0]
    slab = fitting(64, rows)

    @pl.loop(0, rows // slab)
    def _(step):
        body(pl.ds(pl.multiple_of(step * slab, slab), slab))


class Chain:
    def __init__(self, token=None):
        self.token = token

    def call(self, kernel, name, grid, places, ins, outs, aliases=()):
        ins = list(ins)
        n_out = len(outs)
        if self.token is not None:
            ins.append((self.token, any_spec))
        n_in = len(ins)

        def body(place_ref, *refs):
            kernel(place_ref, refs[:n_in], refs[n_in : n_in + n_out])

        got = pl.pallas_call(
            body,
            grid_spec=pltpu.PrefetchScalarGridSpec(
                num_scalar_prefetch=1,
                grid=grid,
                in_specs=[spec for _, spec in ins],
                out_specs=[spec for _, _, spec in outs] + [any_spec],
            ),
            out_shape=[jax.ShapeDtypeStruct(shape, kind) for shape, kind, _ in outs]
            + [jax.ShapeDtypeStruct((8, 128), jnp.float32)],
            input_output_aliases={i + 1: o for i, o in aliases},
            compiler_params=pltpu.CompilerParams(vmem_limit_bytes=64 * 1024 * 1024 - 128 * 1024),
            cost_estimate=pl.CostEstimate(flops=0, bytes_accessed=0, transcendentals=0),
            name=name,
        )(places, *[array for array, _ in ins])
        self.token = got[-1]
        return got[:-1]


def cast_kernel(places, ins, outs):
    def slab(at):
        outs[0][at] = ins[0][at].astype(outs[0].dtype)

    by_slabs(outs[0], slab)


def cast_rows(chain, places, weight, first, size):
    cols = weight.shape[1]
    block = fitting(512, first, size) if first else fitting(size, size)
    if block > 512:
        block = fitting(block // 2, size)
    skip = first // block
    return chain.call(
        cast_kernel,
        "cast_rows",
        (size // block,),
        places,
        [(weight, pl.BlockSpec((block, cols), lambda r, at: (skip + r, 0)))],
        [((size, cols), jnp.bfloat16, pl.BlockSpec((block, cols), lambda r, at: (r, 0)))],
    )[0]


def mask_kernel(places, ins, outs):
    ids, cot = ins[0], ins[1]
    rows, cols = cot.shape
    turned = jnp.broadcast_to(ids[...], (128, rows)).T
    keep = turned != pad_token
    for at in range(0, cols, 128):
        value = cot[:, at : at + 128]
        outs[0][:, at : at + 128] = jnp.where(keep, value, jnp.zeros_like(value))


def mask_rows(chain, places, ids, cot):
    rows, cols = cot.shape
    block = fitting(256, rows)
    return chain.call(
        mask_kernel,
        "mask_rows",
        (rows // block,),
        places,
        [
            (ids, pl.BlockSpec((1, block), lambda r, at: (0, r))),
            (cot, pl.BlockSpec((block, cols), lambda r, at: (r, 0))),
        ],
        [((rows, cols), cot.dtype, pl.BlockSpec((block, cols), lambda r, at: (r, 0)))],
    )[0]


def take_columns(chain, places, features, by, n, half):
    toks = features.shape[0]
    block = fitting(256, toks)
    return chain.call(
        cast_kernel,
        "take_columns",
        (toks // block,),
        places,
        [
            (
                features,
                pl.BlockSpec((block, half), lambda r, at: (r, 2 * lax.rem(at[0] + by, n) + at[1])),
            )
        ],
        [((toks, half), features.dtype, pl.BlockSpec((block, half), lambda r, at: (r, 0)))],
    )[0]


def take_rows(chain, places, weight):
    half, cols = weight.shape[0] // 2, weight.shape[1]
    block = fitting(512, half)
    steps = half // block
    return chain.call(
        cast_kernel,
        "take_rows",
        (steps,),
        places,
        [(weight, pl.BlockSpec((block, cols), lambda r, at: ((1 - at[1]) * steps + r, 0)))],
        [((half, cols), jnp.bfloat16, pl.BlockSpec((block, cols), lambda r, at: (r, 0)))],
    )[0]


def velocity_kernel(n, scale, places, ins, outs):
    total = None
    for x_ref, m_ref in zip(ins[:n], ins[n : 2 * n]):
        term = lax.dot_general(
            x_ref[...], m_ref[...], (((0,), (0,)), ((), ())), preferred_element_type=jnp.float32
        )
        total = term if total is None else total + term
    v = momentum_keep * ins[2 * n][...] + total * scale
    outs[0][...] = v
    outs[1][...] = v.astype(jnp.bfloat16)


def velocity_rows(chain, places, activation, others, masks, momentum, first, size):
    rows, cols = momentum.shape
    toks = activation.shape[0]
    n = len(masks)
    block = fitting(256, first, size)
    per_dev, skip = rows // block, first // block
    row_spec = pl.BlockSpec((block, cols), lambda r, at: (r, 0))
    return chain.call(
        functools.partial(velocity_kernel, n, 1.0 / (toks * n)),
        "velocity_rows",
        (size // block,),
        places,
        [(activation, pl.BlockSpec((toks, block), lambda r, at: (0, at[0] * per_dev + skip + r)))]
        + [(x, pl.BlockSpec((toks, block), lambda r, at: (0, skip + r))) for x in others]
        + [(m, pl.BlockSpec((toks, cols), lambda r, at: (0, 0))) for m in masks]
        + [(momentum, pl.BlockSpec((block, cols), lambda r, at: (skip + r, 0)))],
        [((size, cols), jnp.float32, row_spec), ((size, cols), jnp.bfloat16, row_spec)],
    )


def input_kernel(places, ins, outs):
    own, other = (
        lax.dot_general(
            ins[at][...],
            ins[at + 1][...].astype(jnp.bfloat16),
            (((1,), (1,)), ((), ())),
            preferred_element_type=jnp.float32,
        )
        for at in (0, 2)
    )
    outs[0][...] = (own + other).astype(outs[0].dtype)


def input_columns(chain, places, mask, weight, mask_other, short_other):
    half, cols = short_other.shape
    toks = mask.shape[0]
    block = fitting(256, half)
    steps = half // block
    mask_spec = pl.BlockSpec((toks, cols), lambda r, at: (0, 0))
    return chain.call(
        input_kernel,
        "input_columns",
        (steps,),
        places,
        [
            (mask, mask_spec),
            (weight, pl.BlockSpec((block, cols), lambda r, at: (at[1] * steps + r, 0))),
            (mask_other, mask_spec),
            (short_other, pl.BlockSpec((block, cols), lambda r, at: (r, 0))),
        ],
        [((toks, half), jnp.bfloat16, pl.BlockSpec((toks, block), lambda r, at: (0, r)))],
    )[0]


def join_kernel(n, places, ins, outs):
    column = pl.program_id(0)
    by = lax.rem(column // 2 - places[0] + n, n)
    piece = 2 * by + jnp.where(lax.rem(column, 2) == places[1], 0, 1)
    for at in range(2 * n):

        @pl.when(piece == at)
        def _():

            def slab(rows):
                outs[0][rows] = ins[at][rows]

            by_slabs(outs[0], slab)


def join_columns(chain, places, pieces):
    toks, width = pieces[0].shape
    return chain.call(
        functools.partial(join_kernel, len(pieces) // 2),
        "join_columns",
        (len(pieces),),
        places,
        [(piece, pl.BlockSpec((toks, width), lambda c, at: (0, 0))) for piece in pieces],
        [
            (
                (toks, width * len(pieces)),
                pieces[0].dtype,
                pl.BlockSpec((toks, width), lambda c, at: (0, c)),
            )
        ],
    )[0]


def half_kernel(places, ins, outs):
    def slab(at):
        outs[0][at] = 0.5 * (ins[0][at] + ins[1][at].astype(jnp.float32))

    by_slabs(outs[0], slab)


def half_rows(chain, places, weight, peer, first, into):
    rows, cols = weight.shape
    size = peer.shape[0]
    block = fitting(512, first, size)
    skip = first // block
    whole_spec = pl.BlockSpec((block, cols), lambda r, at: (skip + r, 0))
    ins = [(weight, whole_spec), (peer, pl.BlockSpec((block, cols), lambda r, at: (r, 0)))]
    aliases = []
    if into is not None:
        aliases = [(len(ins), 0)]
        ins.append((into, any_spec))
    return chain.call(
        half_kernel,
        "half_rows",
        (size // block,),
        places,
        ins,
        [((rows, cols), jnp.float32, whole_spec)],
        aliases,
    )[0]


def final_kernel(places, ins, outs):
    def slab(at):
        mean = 0.5 * (ins[0][at] + ins[1][at].astype(jnp.float32))
        outs[1][at] = mean
        outs[0][at] = ins[2][at] - ins[3][0] * mean

    by_slabs(outs[0], slab)


def final_rows(chain, places, rate, v, peer, half, into, first):
    rows, cols = half.shape
    size = v.shape[0]
    block = fitting(256, first, size)
    skip = first // block
    part_spec = pl.BlockSpec((block, cols), lambda r, at: (r, 0))
    whole_spec = pl.BlockSpec((block, cols), lambda r, at: (skip + r, 0))
    ins = [
        (v, part_spec),
        (peer, part_spec),
        (half, whole_spec),
        (rate, pl.BlockSpec(memory_space=pltpu.SMEM)),
    ]
    aliases = [(2, 0)]
    if into is not None:
        aliases.append((len(ins), 1))
        ins.append((into, any_spec))
    return chain.call(
        final_kernel,
        "final_rows",
        (size // block,),
        places,
        ins,
        [((rows, cols), jnp.float32, whole_spec)] * 2,
        aliases,
    )


def step_with(bit, token, first_short, places, rate, ids, activation, cotangent, weight, momentum):
    rows = weight.shape[0]
    n_dp = lax.axis_size("dp")
    mp = places[1]
    half = rows // 2
    chain = Chain(token)

    weight_pieces = starts_of(weight_parts, rows)
    weight_peers = [from_partner(first_short, bit)]
    for first, size in weight_pieces[1:]:
        weight_peers.append(from_partner(cast_rows(chain, places, weight, first, size), bit))

    masked = mask_rows(chain, places, ids, cotangent)
    masks = [masked] + [shifted(masked, "dp", k) for k in range(1, n_dp)]

    others = []
    for k in range(1, n_dp):
        mine = shifted(take_columns(chain, places, activation, k, n_dp, half), "dp", k)
        other = shifted(mine, "mp", 1)
        others.append(
            jnp.where(mp == 0, jnp.concatenate([mine, other], 1), jnp.concatenate([other, mine], 1))
        )

    new_weight = half_rows(chain, places, weight, weight_peers[0], 0, None)
    short_other = shifted(take_rows(chain, places, weight), "mp", 1)

    velocities = []
    for first, size in starts_of(velocity_parts, rows):
        v, v_short = velocity_rows(chain, places, activation, others, masks, momentum, first, size)
        velocities.append((first, v, from_partner(v_short, bit)))

    for (first, _), peer in zip(weight_pieces[1:], weight_peers[1:]):
        new_weight = half_rows(chain, places, weight, peer, first, new_weight)

    done = {}
    for k in reversed(range(n_dp)):
        done[k] = input_columns(
            chain, places, masks[k], weight, shifted(masks[k], "mp", 1), short_other
        )
        if k:
            done[k] = shifted(done[k], "dp", n_dp - k)

    pieces = []
    for k in range(n_dp):
        pieces += [done[k], shifted(done[k], "mp", 1)]
    input_grad = join_columns(chain, places, pieces)

    new_momentum = None
    for first, v, peer in velocities:
        new_weight, new_momentum = final_rows(
            chain, places, rate, v, peer, new_weight, new_momentum, first
        )
    return input_grad, new_weight, new_momentum


def on_device(step_index, token_ids, features, cotangent, weight, momentum):
    bit_count = lax.axis_size("outer").bit_length() - 1
    places = jnp.stack([lax.axis_index("dp"), lax.axis_index("mp")]).astype(jnp.int32)
    rate = (peak_rate * (step_index + 1).astype(jnp.float32) / warm_steps)[None]
    chain = Chain()
    first, size = starts_of(weight_parts, weight.shape[1])[0]
    first_short = cast_rows(chain, places, weight[0], first, size)
    outs = lax.switch(
        step_index % bit_count,
        [functools.partial(step_with, bit) for bit in range(bit_count)],
        chain.token,
        first_short,
        places,
        rate,
        token_ids,
        features[0],
        cotangent[0],
        weight[0],
        momentum[0],
    )
    return tuple(out[None] for out in outs)


def solution(mesh):
    placed = (
        P(),
        P("outer", "dp"),
        P("outer", "dp", None),
        P("outer", "dp", "mp"),
        P("outer", "dp", "mp"),
        P("outer", "dp", "mp"),
    )
    return jax.shard_map(
        on_device,
        mesh=mesh,
        in_specs=placed,
        out_specs=(P("outer", "dp", None), P("outer", "dp", "mp"), P("outer", "dp", "mp")),
        check_vma=False,
    )
```

```python
import functools

import jax
import jax.numpy as jnp
from jax import lax
from jax.experimental import pallas as pl
from jax.experimental.pallas import tpu as pltpu
from jax.sharding import PartitionSpec as P

pad_token = 128004
peak_rate = 0.1
warm_steps = 4096.0
momentum_keep = 0.9

weight_parts = (4, 12)
velocity_parts = (10, 4, 2)
last_cuts = 2

any_spec = pl.BlockSpec(memory_space=pl.ANY)


def shifted(value, axis, by):
    n = lax.axis_size(axis)
    return lax.ppermute(value, axis, [(s, (s + by) % n) for s in range(n)])


def from_partner(value, bit):
    n = lax.axis_size("outer")
    return lax.ppermute(value, "outer", [(s, s ^ (1 << bit)) for s in range(n)])


def starts_of(parts, rows):
    out, at, upto = [], 0, 0
    for part in parts:
        upto += part
        end = -(-rows * upto // (16 * 128)) * 128
        if end > at:
            out.append((at, end - at))
        at = end
    return out


def fitting(largest, *sizes):
    block = largest
    while any(size % block for size in sizes):
        block //= 2
    return block


def by_slabs(ref, body, largest=64):
    rows = ref.shape[0]
    slab = fitting(largest, rows)

    @pl.loop(0, rows // slab)
    def _(step):
        body(pl.ds(pl.multiple_of(step * slab, slab), slab))


class Chain:
    def __init__(self, token=None):
        self.token = token

    def call(self, kernel, name, grid, places, ins, outs, aliases=()):
        ins = list(ins)
        n_out = len(outs)
        if self.token is not None:
            ins.append((self.token, any_spec))
        n_in = len(ins)

        def body(place_ref, *refs):
            kernel(place_ref, refs[:n_in], refs[n_in : n_in + n_out])

        got = pl.pallas_call(
            body,
            grid_spec=pltpu.PrefetchScalarGridSpec(
                num_scalar_prefetch=1,
                grid=grid,
                in_specs=[spec for _, spec in ins],
                out_specs=[spec for _, _, spec in outs] + [any_spec],
            ),
            out_shape=[jax.ShapeDtypeStruct(shape, kind) for shape, kind, _ in outs]
            + [jax.ShapeDtypeStruct((8, 128), jnp.float32)],
            input_output_aliases={i + 1: o for i, o in aliases},
            compiler_params=pltpu.CompilerParams(vmem_limit_bytes=64 * 1024 * 1024 - 128 * 1024),
            cost_estimate=pl.CostEstimate(flops=0, bytes_accessed=0, transcendentals=0),
            name=name,
        )(places, *[array for array, _ in ins])
        self.token = got[-1]
        return got[:-1]


def cast_kernel(places, ins, outs):
    def slab(at):
        outs[0][at] = ins[0][at].astype(outs[0].dtype)

    by_slabs(outs[0], slab)


def cast_rows(chain, places, weight, first, size):
    cols = weight.shape[1]
    block = fitting(512 if first else 256, first, size)
    skip = first // block
    return chain.call(
        cast_kernel,
        "cast_rows",
        (size // block,),
        places,
        [(weight, pl.BlockSpec((block, cols), lambda r, at: (skip + r, 0)))],
        [((size, cols), jnp.bfloat16, pl.BlockSpec((block, cols), lambda r, at: (r, 0)))],
    )[0]


def mask_kernel(places, ins, outs):
    ids, cot = ins[0], ins[1]
    rows, cols = cot.shape
    turned = jnp.broadcast_to(ids[...], (128, rows)).T
    keep = turned != pad_token

    @pl.loop(0, cols // 128)
    def _(step):
        at = pl.ds(pl.multiple_of(step * 128, 128), 128)
        value = cot[:, at]
        outs[0][:, at] = jnp.where(keep, value, jnp.zeros_like(value))


def mask_rows(chain, places, ids, cot):
    rows, cols = cot.shape
    block = fitting(256, rows)
    return chain.call(
        mask_kernel,
        "mask_rows",
        (rows // block,),
        places,
        [
            (ids, pl.BlockSpec((1, block), lambda r, at: (0, r))),
            (cot, pl.BlockSpec((block, cols), lambda r, at: (r, 0))),
        ],
        [((rows, cols), cot.dtype, pl.BlockSpec((block, cols), lambda r, at: (r, 0)))],
    )[0]


def take_columns(chain, places, features, by, n, half):
    toks = features.shape[0]
    block = fitting(256, toks)
    return chain.call(
        cast_kernel,
        "take_columns",
        (toks // block,),
        places,
        [
            (
                features,
                pl.BlockSpec((block, half), lambda r, at: (r, 2 * lax.rem(at[0] + by, n) + at[1])),
            )
        ],
        [((toks, half), features.dtype, pl.BlockSpec((block, half), lambda r, at: (r, 0)))],
    )[0]


def take_rows(chain, places, weight):
    half, cols = weight.shape[0] // 2, weight.shape[1]
    block = fitting(512, half)
    steps = half // block
    return chain.call(
        cast_kernel,
        "take_rows",
        (steps,),
        places,
        [(weight, pl.BlockSpec((block, cols), lambda r, at: ((1 - at[1]) * steps + r, 0)))],
        [((half, cols), jnp.bfloat16, pl.BlockSpec((block, cols), lambda r, at: (r, 0)))],
    )[0]


def velocity_kernel(n, scale, places, ins, outs):
    total = None
    for x_ref, m_ref in zip(ins[:n], ins[n : 2 * n]):
        term = lax.dot_general(
            x_ref[...], m_ref[...], (((0,), (0,)), ((), ())), preferred_element_type=jnp.float32
        )
        total = term if total is None else total + term
    v = momentum_keep * ins[2 * n][...] + total * scale
    outs[0][...] = v
    at = 0
    for out in outs[1:]:
        out[...] = v[at : at + out.shape[0]].astype(jnp.bfloat16)
        at += out.shape[0]


def velocity_rows(chain, places, activation, others, masks, momentum, first, size, cuts):
    rows, cols = momentum.shape
    toks = activation.shape[0]
    n = len(masks)
    block = fitting(256, first, size)
    if block < size:
        cuts = 1
    per_dev, skip = rows // block, first // block
    cut_spec = pl.BlockSpec((block // cuts, cols), lambda r, at: (r, 0))
    row_spec = pl.BlockSpec((block, cols), lambda r, at: (r, 0))
    return chain.call(
        functools.partial(velocity_kernel, n, 1.0 / (toks * n)),
        "velocity_rows",
        (size // block,),
        places,
        [(activation, pl.BlockSpec((toks, block), lambda r, at: (0, at[0] * per_dev + skip + r)))]
        + [(x, pl.BlockSpec((toks, block), lambda r, at: (0, skip + r))) for x in others]
        + [(m, pl.BlockSpec((toks, cols), lambda r, at: (0, 0))) for m in masks]
        + [(momentum, pl.BlockSpec((block, cols), lambda r, at: (skip + r, 0)))],
        [((size, cols), jnp.float32, row_spec)]
        + [((size // cuts, cols), jnp.bfloat16, cut_spec)] * cuts,
    )


def input_kernel(places, ins, outs):
    def slab(at):
        own, other = (
            lax.dot_general(
                ins[i][at],
                ins[i + 1][...].astype(jnp.bfloat16),
                (((1,), (1,)), ((), ())),
                preferred_element_type=jnp.float32,
            )
            for i in (0, 2)
        )
        outs[0][at] = (own + other).astype(outs[0].dtype)

    by_slabs(outs[0], slab, 256)


def input_columns(chain, places, mask, weight, mask_other, short_other):
    half, cols = short_other.shape
    toks = mask.shape[0]
    block = fitting(256, half)
    steps = half // block
    mask_spec = pl.BlockSpec((toks, cols), lambda r, at: (0, 0))
    return chain.call(
        input_kernel,
        "input_columns",
        (steps,),
        places,
        [
            (mask, mask_spec),
            (weight, pl.BlockSpec((block, cols), lambda r, at: (at[1] * steps + r, 0))),
            (mask_other, mask_spec),
            (short_other, pl.BlockSpec((block, cols), lambda r, at: (r, 0))),
        ],
        [((toks, half), jnp.bfloat16, pl.BlockSpec((toks, block), lambda r, at: (0, r)))],
    )[0]


def join_kernel(n, places, ins, outs):
    column = pl.program_id(0)
    by = lax.rem(column // 2 - places[0] + n, n)
    piece = 2 * by + jnp.where(lax.rem(column, 2) == places[1], 0, 1)
    for at in range(2 * n):

        @pl.when(piece == at)
        def _():

            def slab(rows):
                outs[0][rows] = ins[at][rows]

            by_slabs(outs[0], slab)


def join_columns(chain, places, pieces):
    toks, width = pieces[0].shape
    return chain.call(
        functools.partial(join_kernel, len(pieces) // 2),
        "join_columns",
        (len(pieces),),
        places,
        [(piece, pl.BlockSpec((toks, width), lambda c, at: (0, 0))) for piece in pieces],
        [
            (
                (toks, width * len(pieces)),
                pieces[0].dtype,
                pl.BlockSpec((toks, width), lambda c, at: (0, c)),
            )
        ],
    )[0]


def half_kernel(places, ins, outs):
    def slab(at):
        outs[0][at] = 0.5 * (ins[0][at] + ins[1][at].astype(jnp.float32))

    by_slabs(outs[0], slab)


def half_rows(chain, places, weight, peer, first, into):
    rows, cols = weight.shape
    size = peer.shape[0]
    block = fitting(512, first, size)
    skip = first // block
    whole_spec = pl.BlockSpec((block, cols), lambda r, at: (skip + r, 0))
    ins = [(weight, whole_spec), (peer, pl.BlockSpec((block, cols), lambda r, at: (r, 0)))]
    aliases = []
    if into is not None:
        aliases = [(len(ins), 0)]
        ins.append((into, any_spec))
    return chain.call(
        half_kernel,
        "half_rows",
        (size // block,),
        places,
        ins,
        [((rows, cols), jnp.float32, whole_spec)],
        aliases,
    )[0]


def final_kernel(places, ins, outs):
    def slab(at):
        mean = 0.5 * (ins[0][at] + ins[1][at].astype(jnp.float32))
        outs[1][at] = mean
        outs[0][at] = ins[2][at] - ins[3][0] * mean

    by_slabs(outs[0], slab)


def final_rows(chain, places, rate, v, start, peer, half, into, first):
    rows, cols = half.shape
    size = peer.shape[0]
    block = fitting(256, first, start, size)
    v_skip, skip = start // block, (first + start) // block
    part_spec = pl.BlockSpec((block, cols), lambda r, at: (r, 0))
    whole_spec = pl.BlockSpec((block, cols), lambda r, at: (skip + r, 0))
    ins = [
        (v, pl.BlockSpec((block, cols), lambda r, at: (v_skip + r, 0))),
        (peer, part_spec),
        (half, whole_spec),
        (rate, pl.BlockSpec(memory_space=pltpu.SMEM)),
    ]
    aliases = [(2, 0)]
    if into is not None:
        aliases.append((len(ins), 1))
        ins.append((into, any_spec))
    return chain.call(
        final_kernel,
        "final_rows",
        (size // block,),
        places,
        ins,
        [((rows, cols), jnp.float32, whole_spec)] * 2,
        aliases,
    )


def step_with(bit, token, first_short, places, rate, ids, activation, cotangent, weight, momentum):
    rows = weight.shape[0]
    n_dp = lax.axis_size("dp")
    mp = places[1]
    half = rows // 2
    chain = Chain(token)

    weight_pieces = starts_of(weight_parts, rows)
    weight_peers = [from_partner(first_short, bit)]
    for first, size in weight_pieces[1:]:
        weight_peers.append(from_partner(cast_rows(chain, places, weight, first, size), bit))

    masked = mask_rows(chain, places, ids, cotangent)
    masks = [masked] + [shifted(masked, "dp", k) for k in range(1, n_dp)]

    others = []
    for k in range(1, n_dp):
        mine = shifted(take_columns(chain, places, activation, k, n_dp, half), "dp", k)
        other = shifted(mine, "mp", 1)
        others.append(
            jnp.where(mp == 0, jnp.concatenate([mine, other], 1), jnp.concatenate([other, mine], 1))
        )

    new_weight = half_rows(chain, places, weight, weight_peers[0], 0, None)
    short_other = shifted(take_rows(chain, places, weight), "mp", 1)

    velocities = []
    velocity_pieces = starts_of(velocity_parts, rows)
    for first, size in velocity_pieces:
        cuts = last_cuts if first == velocity_pieces[-1][0] else 1
        v, *shorts = velocity_rows(
            chain, places, activation, others, masks, momentum, first, size, cuts
        )
        at = 0
        for v_short in shorts:
            velocities.append((first, v, at, from_partner(v_short, bit)))
            at += v_short.shape[0]

    for (first, _), peer in zip(weight_pieces[1:], weight_peers[1:]):
        new_weight = half_rows(chain, places, weight, peer, first, new_weight)

    done = {}
    for k in reversed(range(n_dp)):
        done[k] = input_columns(
            chain, places, masks[k], weight, shifted(masks[k], "mp", 1), short_other
        )
        if k:
            done[k] = shifted(done[k], "dp", n_dp - k)

    pieces = []
    for k in range(n_dp):
        pieces += [done[k], shifted(done[k], "mp", 1)]
    input_grad = join_columns(chain, places, pieces)

    new_momentum = None
    for first, v, at, peer in velocities:
        new_weight, new_momentum = final_rows(
            chain, places, rate, v, at, peer, new_weight, new_momentum, first
        )
    return input_grad, new_weight, new_momentum


def on_device(step_index, token_ids, features, cotangent, weight, momentum):
    bit_count = lax.axis_size("outer").bit_length() - 1
    places = jnp.stack([lax.axis_index("dp"), lax.axis_index("mp")]).astype(jnp.int32)
    rate = (peak_rate * (step_index + 1).astype(jnp.float32) / warm_steps)[None]
    chain = Chain()
    first, size = starts_of(weight_parts, weight.shape[1])[0]
    first_short = cast_rows(chain, places, weight[0], first, size)
    outs = lax.switch(
        step_index % bit_count,
        [functools.partial(step_with, bit) for bit in range(bit_count)],
        chain.token,
        first_short,
        places,
        rate,
        token_ids,
        features[0],
        cotangent[0],
        weight[0],
        momentum[0],
    )
    return tuple(out[None] for out in outs)


def solution(mesh):
    placed = (
        P(),
        P("outer", "dp"),
        P("outer", "dp", None),
        P("outer", "dp", "mp"),
        P("outer", "dp", "mp"),
        P("outer", "dp", "mp"),
    )
    return jax.shard_map(
        on_device,
        mesh=mesh,
        in_specs=placed,
        out_specs=(P("outer", "dp", None), P("outer", "dp", "mp"), P("outer", "dp", "mp")),
        check_vma=False,
    )
```

```python
import functools

import jax
import jax.numpy as jnp
from jax import lax
from jax.experimental import pallas as pl
from jax.experimental.pallas import tpu as pltpu
from jax.sharding import PartitionSpec as P

pad_token = 128004
peak_rate = 0.1
warm_steps = 4096.0
momentum_keep = 0.9

weight_parts = (4, 12)
velocity_parts = (10, 4, 2)
last_cuts = 2

any_spec = pl.BlockSpec(memory_space=pl.ANY)


def shifted(value, axis, by):
    n = lax.axis_size(axis)
    return lax.ppermute(value, axis, [(s, (s + by) % n) for s in range(n)])


def from_partner(value, bit):
    n = lax.axis_size("outer")
    return lax.ppermute(value, "outer", [(s, s ^ (1 << bit)) for s in range(n)])


def starts_of(parts, rows):
    out, at, upto = [], 0, 0
    for part in parts:
        upto += part
        end = -(-rows * upto // (16 * 128)) * 128
        if end > at:
            out.append((at, end - at))
        at = end
    return out


def fitting(largest, *sizes):
    block = largest
    while any(size % block for size in sizes):
        block //= 2
    return block


def by_slabs(ref, body, largest=64):
    rows = ref.shape[0]
    slab = fitting(largest, rows)

    @pl.loop(0, rows // slab)
    def _(step):
        body(pl.ds(pl.multiple_of(step * slab, slab), slab))


class Chain:
    def __init__(self, token=None):
        self.token = token

    def call(self, kernel, name, grid, places, ins, outs, aliases=()):
        ins = list(ins)
        n_out = len(outs)
        if self.token is not None:
            ins.append((self.token, any_spec))
        n_in = len(ins)
        numbers = [] if places is None else [places]
        lead = len(numbers)

        def body(*refs):
            place_ref = refs[0] if lead else None
            refs = refs[lead:]
            kernel(place_ref, refs[:n_in], refs[n_in : n_in + n_out])

        got = pl.pallas_call(
            body,
            grid_spec=pltpu.PrefetchScalarGridSpec(
                num_scalar_prefetch=lead,
                grid=grid,
                in_specs=[spec for _, spec in ins],
                out_specs=[spec for _, _, spec in outs] + [any_spec],
            ),
            out_shape=[jax.ShapeDtypeStruct(shape, kind) for shape, kind, _ in outs]
            + [jax.ShapeDtypeStruct((8, 128), jnp.float32)],
            input_output_aliases={i + lead: o for i, o in aliases},
            compiler_params=pltpu.CompilerParams(vmem_limit_bytes=64 * 1024 * 1024 - 128 * 1024),
            cost_estimate=pl.CostEstimate(flops=0, bytes_accessed=0, transcendentals=0),
            name=name,
        )(*numbers, *[array for array, _ in ins])
        self.token = got[-1]
        return got[:-1]


def cast_kernel(places, ins, outs):
    def slab(at):
        outs[0][at] = ins[0][at].astype(outs[0].dtype)

    by_slabs(outs[0], slab)


def cast_rows(chain, weight, first, size):
    cols = weight.shape[1]
    block = fitting(512 if first else 256, first, size)
    skip = first // block
    return chain.call(
        cast_kernel,
        "cast_rows",
        (size // block,),
        None,
        [(weight, pl.BlockSpec((block, cols), lambda r: (skip + r, 0)))],
        [((size, cols), jnp.bfloat16, pl.BlockSpec((block, cols), lambda r: (r, 0)))],
    )[0]


def mask_kernel(places, ins, outs):
    ids, cot = ins[0], ins[1]
    rows, cols = cot.shape
    turned = jnp.broadcast_to(ids[...], (128, rows)).T
    keep = turned != pad_token

    @pl.loop(0, cols // 128)
    def _(step):
        at = pl.ds(pl.multiple_of(step * 128, 128), 128)
        value = cot[:, at]
        outs[0][:, at] = jnp.where(keep, value, jnp.zeros_like(value))


def mask_rows(chain, ids, cot):
    rows, cols = cot.shape
    block = fitting(256, rows)
    return chain.call(
        mask_kernel,
        "mask_rows",
        (rows // block,),
        None,
        [
            (ids, pl.BlockSpec((1, block), lambda r: (0, r))),
            (cot, pl.BlockSpec((block, cols), lambda r: (r, 0))),
        ],
        [((rows, cols), cot.dtype, pl.BlockSpec((block, cols), lambda r: (r, 0)))],
    )[0]


def take_columns(chain, places, features, by, n, half):
    toks = features.shape[0]
    block = fitting(256, toks)
    return chain.call(
        cast_kernel,
        "take_columns",
        (toks // block,),
        places,
        [
            (
                features,
                pl.BlockSpec((block, half), lambda r, at: (r, 2 * lax.rem(at[0] + by, n) + at[1])),
            )
        ],
        [((toks, half), features.dtype, pl.BlockSpec((block, half), lambda r, at: (r, 0)))],
    )[0]


def take_rows(chain, places, weight):
    half, cols = weight.shape[0] // 2, weight.shape[1]
    block = fitting(512, half)
    steps = half // block
    return chain.call(
        cast_kernel,
        "take_rows",
        (steps,),
        places,
        [(weight, pl.BlockSpec((block, cols), lambda r, at: ((1 - at[1]) * steps + r, 0)))],
        [((half, cols), jnp.bfloat16, pl.BlockSpec((block, cols), lambda r, at: (r, 0)))],
    )[0]


def velocity_kernel(n, scale, places, ins, outs):
    total = None
    for x_ref, m_ref in zip(ins[:n], ins[n : 2 * n]):
        term = lax.dot_general(
            x_ref[...], m_ref[...], (((0,), (0,)), ((), ())), preferred_element_type=jnp.float32
        )
        total = term if total is None else total + term
    v = momentum_keep * ins[2 * n][...] + total * scale
    outs[0][...] = v
    at = 0
    for out in outs[1:]:
        out[...] = v[at : at + out.shape[0]].astype(jnp.bfloat16)
        at += out.shape[0]


def velocity_rows(chain, places, activation, others, masks, momentum, first, size, cuts):
    rows, cols = momentum.shape
    toks = activation.shape[0]
    n = len(masks)
    block = fitting(256, first, size)
    if block < size:
        cuts = 1
    per_dev, skip = rows // block, first // block
    cut_spec = pl.BlockSpec((block // cuts, cols), lambda r, at: (r, 0))
    row_spec = pl.BlockSpec((block, cols), lambda r, at: (r, 0))
    return chain.call(
        functools.partial(velocity_kernel, n, 1.0 / (toks * n)),
        "velocity_rows",
        (size // block,),
        places,
        [(activation, pl.BlockSpec((toks, block), lambda r, at: (0, at[0] * per_dev + skip + r)))]
        + [(x, pl.BlockSpec((toks, block), lambda r, at: (0, skip + r))) for x in others]
        + [(m, pl.BlockSpec((toks, cols), lambda r, at: (0, 0))) for m in masks]
        + [(momentum, pl.BlockSpec((block, cols), lambda r, at: (skip + r, 0)))],
        [((size, cols), jnp.float32, row_spec)]
        + [((size // cuts, cols), jnp.bfloat16, cut_spec)] * cuts,
    )


def input_kernel(places, ins, outs):
    def slab(at):
        own, other = (
            lax.dot_general(
                ins[i][at],
                ins[i + 1][...].astype(jnp.bfloat16),
                (((1,), (1,)), ((), ())),
                preferred_element_type=jnp.float32,
            )
            for i in (0, 2)
        )
        outs[0][at] = (own + other).astype(outs[0].dtype)

    by_slabs(outs[0], slab, 256)


def input_columns(chain, places, mask, weight, mask_other, short_other):
    half, cols = short_other.shape
    toks = mask.shape[0]
    block = fitting(256, half)
    steps = half // block
    mask_spec = pl.BlockSpec((toks, cols), lambda r, at: (0, 0))
    return chain.call(
        input_kernel,
        "input_columns",
        (steps,),
        places,
        [
            (mask, mask_spec),
            (weight, pl.BlockSpec((block, cols), lambda r, at: (at[1] * steps + r, 0))),
            (mask_other, mask_spec),
            (short_other, pl.BlockSpec((block, cols), lambda r, at: (r, 0))),
        ],
        [((toks, half), jnp.bfloat16, pl.BlockSpec((toks, block), lambda r, at: (0, r)))],
    )[0]


def join_kernel(n, places, ins, outs):
    column = pl.program_id(0)
    by = lax.rem(column // 2 - places[0] + n, n)
    piece = 2 * by + jnp.where(lax.rem(column, 2) == places[1], 0, 1)
    for at in range(2 * n):

        @pl.when(piece == at)
        def _():

            def slab(rows):
                outs[0][rows] = ins[at][rows]

            by_slabs(outs[0], slab)


def join_columns(chain, places, pieces):
    toks, width = pieces[0].shape
    return chain.call(
        functools.partial(join_kernel, len(pieces) // 2),
        "join_columns",
        (len(pieces),),
        places,
        [(piece, pl.BlockSpec((toks, width), lambda c, at: (0, 0))) for piece in pieces],
        [
            (
                (toks, width * len(pieces)),
                pieces[0].dtype,
                pl.BlockSpec((toks, width), lambda c, at: (0, c)),
            )
        ],
    )[0]


def half_kernel(places, ins, outs):
    def slab(at):
        outs[0][at] = 0.5 * (ins[0][at] + ins[1][at].astype(jnp.float32))

    by_slabs(outs[0], slab)


def half_rows(chain, weight, peer, first, into):
    rows, cols = weight.shape
    size = peer.shape[0]
    block = fitting(512, first, size)
    skip = first // block
    whole_spec = pl.BlockSpec((block, cols), lambda r: (skip + r, 0))
    ins = [(weight, whole_spec), (peer, pl.BlockSpec((block, cols), lambda r: (r, 0)))]
    aliases = []
    if into is not None:
        aliases = [(len(ins), 0)]
        ins.append((into, any_spec))
    return chain.call(
        half_kernel,
        "half_rows",
        (size // block,),
        None,
        ins,
        [((rows, cols), jnp.float32, whole_spec)],
        aliases,
    )[0]


def final_kernel(rate, ins, outs):
    def slab(at):
        mean = 0.5 * (ins[0][at] + ins[1][at].astype(jnp.float32))
        outs[1][at] = mean
        outs[0][at] = ins[2][at] - rate[0] * mean

    by_slabs(outs[0], slab)


def final_rows(chain, rate, v, start, peer, half, into, first):
    rows, cols = half.shape
    size = peer.shape[0]
    block = fitting(256, first, start, size)
    v_skip, skip = start // block, (first + start) // block
    part_spec = pl.BlockSpec((block, cols), lambda r, at: (r, 0))
    whole_spec = pl.BlockSpec((block, cols), lambda r, at: (skip + r, 0))
    ins = [
        (v, pl.BlockSpec((block, cols), lambda r, at: (v_skip + r, 0))),
        (peer, part_spec),
        (half, whole_spec),
    ]
    aliases = [(2, 0)]
    if into is not None:
        aliases.append((len(ins), 1))
        ins.append((into, any_spec))
    return chain.call(
        final_kernel,
        "final_rows",
        (size // block,),
        rate,
        ins,
        [((rows, cols), jnp.float32, whole_spec)] * 2,
        aliases,
    )


def step_with(bit, token, first_short, places, rate, ids, activation, cotangent, weight, momentum):
    rows = weight.shape[0]
    n_dp = lax.axis_size("dp")
    mp = places[1]
    half = rows // 2
    chain = Chain(token)

    weight_pieces = starts_of(weight_parts, rows)
    weight_peers = [from_partner(first_short, bit)]
    for first, size in weight_pieces[1:]:
        weight_peers.append(from_partner(cast_rows(chain, weight, first, size), bit))

    masked = mask_rows(chain, ids, cotangent)
    masks = [masked] + [shifted(masked, "dp", k) for k in range(1, n_dp)]

    others = []
    for k in range(1, n_dp):
        mine = shifted(take_columns(chain, places, activation, k, n_dp, half), "dp", k)
        other = shifted(mine, "mp", 1)
        others.append(
            jnp.where(mp == 0, jnp.concatenate([mine, other], 1), jnp.concatenate([other, mine], 1))
        )

    new_weight = half_rows(chain, weight, weight_peers[0], 0, None)
    short_other = shifted(take_rows(chain, places, weight), "mp", 1)

    velocities = []
    velocity_pieces = starts_of(velocity_parts, rows)
    for first, size in velocity_pieces:
        cuts = last_cuts if first == velocity_pieces[-1][0] else 1
        v, *shorts = velocity_rows(
            chain, places, activation, others, masks, momentum, first, size, cuts
        )
        at = 0
        for v_short in shorts:
            velocities.append((first, v, at, from_partner(v_short, bit)))
            at += v_short.shape[0]

    for (first, _), peer in zip(weight_pieces[1:], weight_peers[1:]):
        new_weight = half_rows(chain, weight, peer, first, new_weight)

    done = {}
    for k in reversed(range(n_dp)):
        done[k] = input_columns(
            chain, places, masks[k], weight, shifted(masks[k], "mp", 1), short_other
        )
        if k:
            done[k] = shifted(done[k], "dp", n_dp - k)

    pieces = []
    for k in range(n_dp):
        pieces += [done[k], shifted(done[k], "mp", 1)]
    input_grad = join_columns(chain, places, pieces)

    new_momentum = None
    for first, v, at, peer in velocities:
        new_weight, new_momentum = final_rows(
            chain, rate, v, at, peer, new_weight, new_momentum, first
        )
    return input_grad, new_weight, new_momentum


def on_device(step_index, token_ids, features, cotangent, weight, momentum):
    bit_count = lax.axis_size("outer").bit_length() - 1
    places = jnp.stack([lax.axis_index("dp"), lax.axis_index("mp")]).astype(jnp.int32)
    rate = (peak_rate * (step_index + 1).astype(jnp.float32) / warm_steps)[None]
    chain = Chain()
    first, size = starts_of(weight_parts, weight.shape[1])[0]
    first_short = cast_rows(chain, weight[0], first, size)
    outs = lax.switch(
        step_index % bit_count,
        [functools.partial(step_with, bit) for bit in range(bit_count)],
        chain.token,
        first_short,
        places,
        rate,
        token_ids,
        features[0],
        cotangent[0],
        weight[0],
        momentum[0],
    )
    return tuple(out[None] for out in outs)


def solution(mesh):
    placed = (
        P(),
        P("outer", "dp"),
        P("outer", "dp", None),
        P("outer", "dp", "mp"),
        P("outer", "dp", "mp"),
        P("outer", "dp", "mp"),
    )
    return jax.shard_map(
        on_device,
        mesh=mesh,
        in_specs=placed,
        out_specs=(P("outer", "dp", None), P("outer", "dp", "mp"), P("outer", "dp", "mp")),
        check_vma=False,
    )
```
